128 devices in a mesh: island: 2 (over y_lo), fsdp: 64 (over y_hi, z, x, core).
Axes of the slice: x: 4, y: 4 (y_hi: 2, y_lo: 2; y = y_hi * 2 + y_lo), z: 4, core: 2. Of those that a mesh axis runs over, the one named last changes fastest.
Arguments:
- tokens: bfloat16 [2, 1024, 8192], P('island', 'fsdp'), may hold values from -6 to 6
- hidden_grad: bfloat16 [2, 1024, 16384], P('island', None, 'fsdp'), may hold values from -1.5 to 1.5
- gate_weight: bfloat16 [2, 8192, 16384], P('island', None, 'fsdp'), as said below
- up_weight: bfloat16 [2, 8192, 16384], P('island', None, 'fsdp'), as said below
- momentum: bfloat16 [2, 8192, 16384], P(None, ('island', 'fsdp')), may hold values from -6 to 6
- layouts: int32 [2, 128], replicated, may hold values from 0 to 127, as said below
Outputs:
- gate_update: bfloat16 [2, 8192, 16384], P('island', None, 'fsdp')
- up_update: bfloat16 [2, 8192, 16384], P('island', None, 'fsdp')
- new_momentum: bfloat16 [2, 8192, 16384], P(None, ('island', 'fsdp'))
The draws below stay inside these ranges and needn't reach their ends.
Inputs may be any that keep to these rules, and one draw needn't show every extreme that they name: Each row of layouts orders all 128 blocks. Device j of fsdp in island i holds blocks layouts[i, j * 2] to layouts[i, (j + 1) * 2 - 1], in that order, as its columns of gate_weight, up_weight, hidden_grad and the updates. gate_weight[i] is the same matrix for every island i, its column blocks in island i's order. up_weight[i] is the same matrix for every island i, its column blocks in island i's order.
All inputs are finite; a program needn't handle non-finite values.
Results may differ from the reference program's by a relative error of at most 0.011.
Values may be sent and summed in bfloat16 or wider, within the bound.
A program may use at most 128 MiB of HBM per device.

```python
import jax
import jax.numpy as jnp
from jax import lax

D = 8192
FFW = 16384
BLOCK = 128
TOK = 1024
NB = 128
N_ISLAND = 2


def shared_layouts(key):
    orders = [jax.random.permutation(jax.random.fold_in(key, 50 + island), NB) for island in range(N_ISLAND)]
    return jnp.stack(orders).astype(jnp.int32)


def spread_columns(base, table):
    units = (table[:, :, None] * BLOCK + jnp.arange(BLOCK, dtype=jnp.int32)[None, None, :]).reshape(N_ISLAND, FFW)
    narrow = base.astype(jnp.bfloat16)
    return jnp.stack([jnp.take(narrow, units[island], axis=1) for island in range(N_ISLAND)])


def draw_layouts(key, part):
    return shared_layouts(key)


def draw_gate_weight(key, part):
    table = shared_layouts(key)
    key = jax.random.fold_in(key, 1)
    base = jax.random.normal(key, (D, FFW), jnp.float32) * D ** (-0.5)
    return spread_columns(base, table)


def draw_up_weight(key, part):
    table = shared_layouts(key)
    key = jax.random.fold_in(key, 2)
    base = jax.random.normal(key, (D, FFW), jnp.float32) * D ** (-0.5)
    return spread_columns(base, table)


def level_of(own_key, extent, cuts, smallest, largest):
    def one(axis_at, shards_of):
        draws = jax.random.uniform(jax.random.fold_in(jax.random.fold_in(own_key, 6), axis_at), (shards_of,), jnp.float32, smallest / len(cuts), largest / len(cuts))
        return jnp.repeat(jnp.exp(draws), extent[axis_at] // shards_of).reshape((-1,) + (1,) * (len(extent) - axis_at - 1))

    gain = one(*cuts[0])
    for cut in cuts[1:]:
        gain = gain * one(*cut)
    return gain


def normal_values(rng, extent, width, most, pieces=(), held_as=jnp.bfloat16):
    array = jax.random.normal(rng, extent, jnp.float32) * width
    if len(pieces) > 0:
        array = level_of(rng, extent, pieces, -0.22, 0.18) * array
    return jnp.clip(array, min=-most, max=most).astype(held_as)


def setup_inputs(seed: int = 0) -> dict:
    key_of = jax.random.split(jax.random.key(seed), 7)
    return {
        "tokens": normal_values(key_of[0], (N_ISLAND, TOK, D), 1.0, 6.0, ((0, 2), (1, 64))),
        "hidden_grad": normal_values(key_of[1], (N_ISLAND, TOK, FFW), 0.25, 1.5, ((0, 2), (2, 64))),
        "gate_weight": draw_gate_weight(jax.random.fold_in(key_of[6], 71), 0),
        "up_weight": draw_up_weight(jax.random.fold_in(key_of[6], 71), 0),
        "momentum": normal_values(key_of[4], (2, D, FFW), 1.0, 6.0, ((1, 128),)),
        "layouts": draw_layouts(jax.random.fold_in(key_of[6], 71), 0),
    }


inner_rate = 0.25
outer_rate = 0.7
momentum_decay = 0.9


def cotangents(gate_pre, up_pre, upstream):
    logistic = jax.nn.sigmoid(gate_pre)
    upstream_wide = upstream.astype(jnp.float32)
    d_gate = (upstream_wide * up_pre * logistic * (1.0 + gate_pre * (1.0 - logistic))).astype(jnp.bfloat16)
    d_up = (upstream_wide * gate_pre * logistic).astype(jnp.bfloat16)
    return d_gate, d_up


def reference(tokens, hidden_grad, gate_weight, up_weight, momentum, layouts):
    contract = (((0,), (0,)), ((), ()))
    summed = jnp.zeros((2, D, FFW), jnp.float32)
    for island in range(N_ISLAND):
        rows = tokens[island]
        gate_pre = jnp.dot(rows, gate_weight[island], preferred_element_type=jnp.float32)
        up_pre = jnp.dot(rows, up_weight[island], preferred_element_type=jnp.float32)
        d_gate, d_up = cotangents(gate_pre, up_pre, hidden_grad[island])
        pseudo_gate = (inner_rate * lax.dot_general(rows, d_gate, contract, preferred_element_type=jnp.float32)).astype(jnp.bfloat16)
        pseudo_up = (inner_rate * lax.dot_general(rows, d_up, contract, preferred_element_type=jnp.float32)).astype(jnp.bfloat16)
        inverse = jnp.argsort(layouts[island]).astype(jnp.int32)
        stacked = jnp.stack([pseudo_gate, pseudo_up]).reshape(2, D, NB, BLOCK)
        canonical = jnp.take(stacked, inverse, axis=2).reshape(2, D, FFW)
        summed = summed + canonical.astype(jnp.float32)
    average = summed / N_ISLAND
    state = momentum_decay * momentum.astype(jnp.float32) + average
    update = (outer_rate * (average + momentum_decay * state)).astype(jnp.bfloat16)
    arranged = update.reshape(2, D, NB, BLOCK)
    gate_parts = []
    up_parts = []
    for island in range(N_ISLAND):
        picked = jnp.take(arranged, layouts[island].astype(jnp.int32), axis=2).reshape(2, D, FFW)
        gate_parts.append(picked[0])
        up_parts.append(picked[1])
    return jnp.stack(gate_parts), jnp.stack(up_parts), state.astype(jnp.bfloat16)
```

```python
import jax
import jax.numpy as jnp
from jax import lax
from jax.experimental import pallas as pl
from jax.experimental.pallas import tpu as pltpu
from jax.sharding import PartitionSpec as P

BLOCK = 128
BY_MESH = pl.DeviceIdType.MESH

inner_rate = 0.25
outer_rate = 0.7
momentum_decay = 0.9

ISLANDS = 2
MEMBERS = 64
PEERS = ISLANDS * MEMBERS
CHIPS = PEERS // 2
ROWS = 64
OWN_TOKENS = 16
STRIDE = 91


def position():
    island = lax.axis_index("island")
    member = lax.axis_index("fsdp")
    return (member // 32) * 2 + island, (member // 8) % 4, (member // 2) % 4, member % 2


def member_of(y, z, x, core):
    return (y // 2) * 32 + z * 8 + x * 2 + core


def slot(far, sibling, near, half):
    return ((far * 2 + sibling) * 4 + near) * 2 + half


def cotangents(gate_pre, up_pre, upstream):
    logistic = jax.nn.sigmoid(gate_pre)
    d_gate = upstream * up_pre * logistic * (1.0 + gate_pre * (1.0 - logistic))
    d_up = upstream * gate_pre * logistic
    return d_gate.astype(jnp.bfloat16), d_up.astype(jnp.bfloat16)


def kernel(
    tokens_ref,
    hidden_ref,
    gate_ref,
    up_ref,
    momentum_ref,
    layout_ref,
    inverse_ref,
    gate_out,
    up_out,
    momentum_out,
    tokens,
    weights,
    hidden,
    cotangent,
    outgoing,
    received,
    momentum,
    update,
    gate_sum,
    up_sum,
    load_sem,
    hidden_sem,
    tokens_sem,
    gather_sent,
    gather_got,
    sums_sent,
    sums_got,
    own_sem,
    updates_sent,
    gate_got,
    up_got,
):
    y, z, x, core = position()
    island = lax.axis_index("island")
    member = lax.axis_index("fsdp")
    me = island * MEMBERS + member

    def partner(step):
        dy, dz, dx, dc = step // 32, (step // 8) % 4, (step // 2) % 4, step % 2
        there_y = (y + dy) % 4
        there = member_of(there_y, (z + dz) % 4, (x + dx) % 4, (core + dc) % 2)
        return there_y % 2, there

    barrier = pltpu.get_barrier_semaphore()

    def greet(step, carry):
        pl.semaphore_signal(barrier, inc=1, device_id=partner(step), device_id_type=BY_MESH)
        return carry

    lax.fori_loop(1, PEERS, greet, 0)

    loads = [
        pltpu.make_async_copy(gate_ref, weights.at[0], load_sem.at[0]),
        pltpu.make_async_copy(up_ref, weights.at[1], load_sem.at[1]),
        pltpu.make_async_copy(momentum_ref, momentum, load_sem.at[2]),
    ]
    own_tokens = pltpu.make_async_copy(tokens_ref, tokens.at[0], tokens_sem)
    own_tokens.start()

    def load_hidden(place, carry):
        half, near, sibling, far = place % 2, (place // 2) % 4, (place // 8) % 2, place // 16
        their_core = (core + sibling) % 2
        dx = near * (1 - their_core) + far * their_core
        dz = near * their_core + far * (1 - their_core)
        there = member_of((y + 2 * half) % 4, (z + dz) % 4, (x + dx) % 4, their_core)
        rows = pl.ds(pl.multiple_of(there * OWN_TOKENS, OWN_TOKENS), OWN_TOKENS)
        pltpu.make_async_copy(hidden_ref.at[rows], hidden.at[place], hidden_sem).start()
        return carry

    lax.fori_loop(0, MEMBERS, load_hidden, 0)
    for load in loads:
        load.start()

    pl.semaphore_wait(barrier, PEERS - 1)

    def along_near(sign):
        return member_of(y, (z + sign * core + 4) % 4, (x + sign * (1 - core) + 4) % 4, core)

    def along_far(sign):
        return member_of(y, (z + sign * (1 - core) + 4) % 4, (x + sign * core + 4) % 4, core)

    other_plane = member_of((y + 2) % 4, z, x, core)
    other_core = member_of(y, z, x, 1 - core)

    def send_tokens(source, place, to):
        pltpu.make_async_remote_copy(
            src_ref=source,
            dst_ref=tokens.at[place],
            send_sem=gather_sent,
            recv_sem=gather_got.at[place],
            device_id=(island, to),
            device_id_type=BY_MESH,
        ).start()

    def arrived(place):
        pltpu.make_async_copy(tokens.at[place], tokens.at[place], gather_got.at[place]).wait()

    def spread(source, near, half):
        send_tokens(source, slot(3, 0, near, half), along_far(1))
        send_tokens(source, slot(1, 0, near, half), along_far(-1))
        send_tokens(source, slot(0, 1, near, half), other_core)

    def ring(source, half):
        send_tokens(source, slot(0, 0, 3, half), along_near(1))
        send_tokens(source, slot(0, 0, 1, half), along_near(-1))

    send_tokens(tokens_ref, slot(0, 0, 0, 1), other_plane)
    ring(tokens_ref, 0)
    spread(tokens_ref, 0, 0)

    place = slot(0, 0, 0, 1)
    arrived(place)
    ring(tokens.at[place], 1)
    spread(tokens.at[place], 0, 1)
    for half in range(2):
        before, after = slot(0, 0, 3, half), slot(0, 0, 1, half)
        arrived(before)
        if half == 0:
            send_tokens(tokens.at[before], slot(0, 0, 2, 0), along_near(1))
        arrived(after)
        if half == 1:
            send_tokens(tokens.at[after], slot(0, 0, 2, 1), along_near(-1))
        spread(tokens.at[before], 3, half)
        spread(tokens.at[after], 1, half)
    for half in range(2):
        place = slot(0, 0, 2, half)
        arrived(place)
        spread(tokens.at[place], 2, half)

    def forward(far):
        depth = 1024
        for part in range(8):
            cols = pl.ds(part * depth, depth)
            rows = tokens[pl.ds(far * 16, 16), :, cols].reshape(256, depth)
            gate_part = jnp.dot(rows, weights[0, cols, :], preferred_element_type=jnp.float32)
            up_part = jnp.dot(rows, weights[1, cols, :], preferred_element_type=jnp.float32)
            if part == 0:
                gate_sum[...] = gate_part
                up_sum[...] = up_part
            else:
                gate_sum[...] += gate_part
                up_sum[...] += up_part
        upstream = hidden[pl.ds(far * 16, 16)].reshape(256, 256).astype(jnp.float32)
        d_gate, d_up = cotangents(gate_sum[...], up_sum[...], upstream)
        cotangent[pl.ds(far * 256, 256), 0:256] = d_gate
        cotangent[pl.ds(far * 256, 256), 256:512] = d_up

    own_tokens.wait()
    loads[0].wait()
    loads[1].wait()
    pltpu.make_async_copy(hidden, hidden, hidden_sem).wait()
    for near in range(4):
        for half in range(2):
            arrived(slot(0, 1, near, half))
    forward(0)

    order = [(0, 0), (0, 1), (1, 0), (3, 0), (1, 1), (3, 1), (2, 0), (2, 1)]
    for near, half in order:
        before, after = slot(3, 0, near, half), slot(1, 0, near, half)
        arrived(before)
        if half == 0:
            send_tokens(tokens.at[before], slot(2, 0, near, 0), along_far(1))
        send_tokens(tokens.at[before], slot(3, 1, near, half), other_core)
        arrived(after)
        if half == 1:
            send_tokens(tokens.at[after], slot(2, 0, near, 1), along_far(-1))
        send_tokens(tokens.at[after], slot(1, 1, near, half), other_core)
    for far in (3, 1):
        for near, half in order:
            arrived(slot(far, 1, near, half))
        forward(far)
    for near, half in order:
        place = slot(2, 0, near, half)
        arrived(place)
        send_tokens(tokens.at[place], slot(2, 1, near, half), other_core)
    for near, half in order:
        arrived(slot(2, 1, near, half))
    forward(2)

    def backward(group, carry):
        steps = [((group * 4 + k) * STRIDE) % CHIPS for k in range(4)]
        chips = []
        for step in steps:
            there_island, there = partner(step * 2)
            chips.append(there_island * 32 + there // 2)
        columns = [
            tokens[:, :, pl.ds(pl.multiple_of(chip * BLOCK, BLOCK), BLOCK)].reshape(1024, BLOCK)
            for chip in chips
        ]
        summed = lax.dot_general(
            jnp.concatenate(columns, axis=1),
            cotangent[...],
            (((0,), (0,)), ((), ())),
            preferred_element_type=jnp.float32,
        )
        scaled = (inner_rate * summed).astype(jnp.bfloat16)
        for k in range(4):
            for half in range(2):
                first = k * BLOCK + half * ROWS
                for part in range(4):
                    matrix, block = part // 2, part % 2
                    outgoing[(chips[k] * 2 + half) * 2 + block, matrix] = scaled[
                        first : first + ROWS, part * BLOCK : (part + 1) * BLOCK
                    ]
        for k in range(4):
            for dc in range(2):
                there_island, there = partner(steps[k] * 2 + dc)
                number = there_island * MEMBERS + there

                @pl.when(number != me)
                def _():
                    pltpu.make_async_remote_copy(
                        src_ref=outgoing.at[pl.ds(number * 2, 2)],
                        dst_ref=received.at[pl.ds(me * 2, 2)],
                        send_sem=sums_sent,
                        recv_sem=sums_got,
                        device_id=(there_island, there),
                        device_id_type=BY_MESH,
                    ).start()

        return carry

    lax.fori_loop(0, CHIPS // 4, backward, 0)
    received[pl.ds(me * 2, 2)] = outgoing[pl.ds(me * 2, 2)]
    loads[2].wait()
    others = received.at[pl.ds(0, (PEERS - 1) * 2)]
    pltpu.make_async_copy(others, others, sums_got).wait()

    def outer_step(block, carry):
        first = inverse_ref[0, block]
        second = inverse_ref[1, block]
        cols = pl.ds(pl.multiple_of(block * BLOCK, BLOCK), BLOCK)
        for matrix in range(2):
            one = received[first, matrix].astype(jnp.float32)
            two = received[second, matrix].astype(jnp.float32)
            average = (one + two) * (1.0 / ISLANDS)
            state = momentum_decay * momentum[matrix, :, cols].astype(jnp.float32) + average
            momentum[matrix, :, cols] = state.astype(jnp.bfloat16)
            update[block, matrix] = (outer_rate * (average + momentum_decay * state)).astype(
                jnp.bfloat16
            )
        return carry

    lax.fori_loop(0, PEERS, outer_step, 0)
    keep = pltpu.make_async_copy(momentum, momentum_out, load_sem.at[2])
    keep.start()

    mine = pl.ds(pl.multiple_of(me * ROWS, ROWS), ROWS)

    def stage(number, there_island, there):
        rows = pl.ds(pl.multiple_of(number * ROWS, ROWS), ROWS)
        for half in range(2):
            block = layout_ref[there_island, there * 2 + half]
            for matrix in range(2):
                weights[matrix, rows, half * BLOCK : (half + 1) * BLOCK] = update[block, matrix]
        return rows

    def give_back(index, carry):
        step = (index * STRIDE) % PEERS
        there_island, there = partner(step)
        rows = stage(there_island * MEMBERS + there, there_island, there)
        for matrix, (out, got) in enumerate(((gate_out, gate_got), (up_out, up_got))):
            pltpu.make_async_remote_copy(
                src_ref=weights.at[matrix, rows],
                dst_ref=out.at[mine],
                send_sem=updates_sent,
                recv_sem=got,
                device_id=(there_island, there),
                device_id_type=BY_MESH,
            ).start()
        return carry

    lax.fori_loop(1, PEERS, give_back, 0)
    stage(me, island, member)
    own = [
        pltpu.make_async_copy(weights.at[0, mine], gate_out.at[mine], own_sem.at[0]),
        pltpu.make_async_copy(weights.at[1, mine], up_out.at[mine], own_sem.at[1]),
    ]
    for copy in own:
        copy.start()
    for copy in own:
        copy.wait()
    keep.wait()
    sent = tokens.at[pl.ds(0, 63)]
    pltpu.make_async_copy(sent, sent, gather_sent).wait()
    pltpu.make_async_copy(others, others, sums_sent).wait()
    for out, got in ((gate_out, gate_got), (up_out, up_got)):
        part = out.at[pl.ds(0, (PEERS - 1) * ROWS)]
        pltpu.make_async_copy(part, part, got).wait()
    pltpu.make_async_copy(others, others, updates_sent).wait()


def shards(tokens, hidden_grad, gate_weight, up_weight, momentum, layouts):
    blocks = layouts.shape[1]
    places = jnp.arange(blocks, dtype=jnp.int32)
    hit = layouts[:, :, None] == places[None, None, :]
    inverse = jnp.sum(jnp.where(hit, places[None, :, None], 0), axis=1, dtype=jnp.int32)
    inverse = inverse + jnp.arange(ISLANDS, dtype=jnp.int32)[:, None] * blocks
    anywhere = pl.BlockSpec(memory_space=pl.ANY)
    scalars = pl.BlockSpec(memory_space=pltpu.SMEM)
    bf16 = jnp.bfloat16
    gate, up, state = pl.pallas_call(
        kernel,
        out_shape=(
            jax.ShapeDtypeStruct((8192, 256), bf16),
            jax.ShapeDtypeStruct((8192, 256), bf16),
            jax.ShapeDtypeStruct((2, ROWS, 16384), bf16),
        ),
        in_specs=[anywhere] * 5 + [scalars] * 2,
        out_specs=(anywhere, anywhere, anywhere),
        scratch_shapes=[
            pltpu.VMEM((MEMBERS, OWN_TOKENS, 8192), bf16),
            pltpu.VMEM((2, 8192, 256), bf16),
            pltpu.VMEM((MEMBERS, OWN_TOKENS, 256), bf16),
            pltpu.VMEM((1024, 512), bf16),
            pltpu.VMEM((PEERS * 2, 2, ROWS, BLOCK), bf16),
            pltpu.VMEM((PEERS * 2, 2, ROWS, BLOCK), bf16),
            pltpu.VMEM((2, ROWS, 16384), bf16),
            pltpu.VMEM((PEERS, 2, ROWS, BLOCK), bf16),
            pltpu.VMEM((256, 256), jnp.float32),
            pltpu.VMEM((256, 256), jnp.float32),
            pltpu.SemaphoreType.DMA((3,)),
            pltpu.SemaphoreType.DMA,
            pltpu.SemaphoreType.DMA,
            pltpu.SemaphoreType.DMA,
            pltpu.SemaphoreType.DMA((64,)),
            pltpu.SemaphoreType.DMA,
            pltpu.SemaphoreType.DMA,
            pltpu.SemaphoreType.DMA((2,)),
            pltpu.SemaphoreType.DMA,
            pltpu.SemaphoreType.DMA,
            pltpu.SemaphoreType.DMA,
        ],
        compiler_params=pltpu.CompilerParams(
            collective_id=0, has_side_effects=True, vmem_limit_bytes=62 * 2**20
        ),
    )(tokens[0], hidden_grad[0], gate_weight[0], up_weight[0], momentum, layouts, inverse)
    return gate[None], up[None], state


def solution(mesh):
    placed = (
        P("island", "fsdp", None),
        P("island", None, "fsdp"),
        P("island", None, "fsdp"),
        P("island", None, "fsdp"),
        P(None, ("island", "fsdp"), None),
        P(),
    )
    return jax.shard_map(
        shards,
        mesh=mesh,
        in_specs=placed,
        out_specs=(
            P("island", None, "fsdp"),
            P("island", None, "fsdp"),
            P(None, ("island", "fsdp"), None),
        ),
        check_vma=False,
    )
```

```python
import jax
import jax.numpy as jnp
from jax import lax
from jax.experimental import pallas as pl
from jax.experimental.pallas import tpu as pltpu
from jax.sharding import PartitionSpec as P

BLOCK = 128
BY_MESH = pl.DeviceIdType.MESH

inner_rate = 0.25
outer_rate = 0.7
momentum_decay = 0.9

ISLANDS = 2
MEMBERS = 64
PEERS = ISLANDS * MEMBERS
CHIPS = PEERS // 2
ROWS = 64
OWN_TOKENS = 16
STRIDE = 91
CHIP_STRIDE = 29


def position():
    island = lax.axis_index("island")
    member = lax.axis_index("fsdp")
    return (member // 32) * 2 + island, (member // 8) % 4, (member // 2) % 4, member % 2


def member_of(y, z, x, core):
    return (y // 2) * 32 + z * 8 + x * 2 + core


def slot(far, sibling, near, half):
    return ((far * 2 + sibling) * 4 + near) * 2 + half


def cotangents(gate_pre, up_pre, upstream):
    logistic = jax.nn.sigmoid(gate_pre)
    d_gate = upstream * up_pre * logistic * (1.0 + gate_pre * (1.0 - logistic))
    d_up = upstream * gate_pre * logistic
    return d_gate.astype(jnp.bfloat16), d_up.astype(jnp.bfloat16)


def kernel(
    tokens_ref,
    hidden_ref,
    gate_ref,
    up_ref,
    momentum_ref,
    layout_ref,
    inverse_ref,
    gate_out,
    up_out,
    momentum_out,
    tokens,
    weights,
    hidden,
    cotangent,
    outgoing,
    gate_received,
    up_received,
    update,
    gate_sum,
    up_sum,
    load_sem,
    hidden_sem,
    tokens_sem,
    gather_sent,
    gather_got,
    sums_sent,
    sums_got,
    own_sem,
    updates_sent,
    updates_got,
    ready,
):
    received = (gate_received, up_received)
    y, z, x, core = position()
    island = lax.axis_index("island")
    member = lax.axis_index("fsdp")
    me = island * MEMBERS + member

    def partner(step):
        dy, dz, dx, dc = step // 32, (step // 8) % 4, (step // 2) % 4, step % 2
        there_y = (y + dy) % 4
        there = member_of(there_y, (z + dz) % 4, (x + dx) % 4, (core + dc) % 2)
        return there_y % 2, there

    near_plus, near_minus, far_plus, far_minus = (
        member_of(y, (z + dz) % 4, (x + dx) % 4, core)
        for dz, dx in (
            (core, 1 - core),
            (3 * core, 3 * (1 - core)),
            (1 - core, core),
            (3 * (1 - core), 3 * core),
        )
    )
    other_plane = member_of((y + 2) % 4, z, x, core)
    other_core = member_of(y, z, x, 1 - core)
    above, below = (y + 1) % 4, (y + 3) % 4
    barrier = pltpu.get_barrier_semaphore()
    greeted = [(island, near_plus), (island, near_minus), (island, far_plus), (island, far_minus)]
    greeted += [(island, other_plane), (island, other_core)]
    greeted += [(below % 2, member_of(below, z, x, core))]
    for there in greeted:
        pl.semaphore_signal(barrier, inc=1, device_id=there, device_id_type=BY_MESH)

    loads = [
        pltpu.make_async_copy(gate_ref, weights.at[0], load_sem.at[0]),
        pltpu.make_async_copy(up_ref, weights.at[1], load_sem.at[1]),
        pltpu.make_async_copy(momentum_ref, momentum_out, load_sem.at[2]),
    ]
    own_tokens = pltpu.make_async_copy(tokens_ref, tokens.at[0], tokens_sem)
    own_tokens.start()

    def load_hidden(place, carry):
        half, near, sibling, far = place % 2, (place // 2) % 4, (place // 8) % 2, place // 16
        their_core = (core + sibling) % 2
        dx = near * (1 - their_core) + far * their_core
        dz = near * their_core + far * (1 - their_core)
        there = member_of((y + 2 * half) % 4, (z + dz) % 4, (x + dx) % 4, their_core)
        rows = pl.ds(pl.multiple_of(there * OWN_TOKENS, OWN_TOKENS), OWN_TOKENS)
        pltpu.make_async_copy(hidden_ref.at[rows], hidden.at[place], hidden_sem).start()
        return carry

    lax.fori_loop(0, MEMBERS, load_hidden, 0)
    for load in loads:
        load.start()

    pl.semaphore_wait(barrier, len(greeted))

    def send_tokens(source, place, to):
        pltpu.make_async_remote_copy(
            src_ref=source,
            dst_ref=tokens.at[place],
            send_sem=gather_sent,
            recv_sem=gather_got.at[place],
            device_id=(island, to),
            device_id_type=BY_MESH,
        ).start()

    def arrived(place):
        pltpu.make_async_copy(tokens.at[place], tokens.at[place], gather_got.at[place]).wait()

    def spread(source, near, half):
        send_tokens(source, slot(3, 0, near, half), far_plus)
        send_tokens(source, slot(1, 0, near, half), far_minus)
        send_tokens(source, slot(0, 1, near, half), other_core)

    def ring(source, half):
        send_tokens(source, slot(0, 0, 3, half), near_plus)
        send_tokens(source, slot(0, 0, 1, half), near_minus)

    send_tokens(tokens_ref, slot(0, 0, 0, 1), other_plane)
    ring(tokens_ref, 0)
    spread(tokens_ref, 0, 0)

    place = slot(0, 0, 0, 1)
    arrived(place)
    ring(tokens.at[place], 1)
    spread(tokens.at[place], 0, 1)
    for half in range(2):
        before, after = slot(0, 0, 3, half), slot(0, 0, 1, half)
        arrived(before)
        if half == 0:
            send_tokens(tokens.at[before], slot(0, 0, 2, 0), near_plus)
        arrived(after)
        if half == 1:
            send_tokens(tokens.at[after], slot(0, 0, 2, 1), near_minus)
        spread(tokens.at[before], 3, half)
        spread(tokens.at[after], 1, half)
    for half in range(2):
        place = slot(0, 0, 2, half)
        arrived(place)
        spread(tokens.at[place], 2, half)

    def forward(far):
        depth = 1024
        for part in range(8):
            cols = pl.ds(part * depth, depth)
            rows = tokens[pl.ds(far * 16, 16), :, cols].reshape(256, depth)
            gate_part = jnp.dot(rows, weights[0, cols, :], preferred_element_type=jnp.float32)
            up_part = jnp.dot(rows, weights[1, cols, :], preferred_element_type=jnp.float32)
            if part == 0:
                gate_sum[...] = gate_part
                up_sum[...] = up_part
            else:
                gate_sum[...] += gate_part
                up_sum[...] += up_part
        upstream = hidden[pl.ds(far * 16, 16)].reshape(256, 256).astype(jnp.float32)
        d_gate, d_up = cotangents(gate_sum[...], up_sum[...], upstream)
        cotangent[pl.ds(far * 256, 256), 0:256] = d_gate
        cotangent[pl.ds(far * 256, 256), 256:512] = d_up

    own_tokens.wait()
    loads[0].wait()
    loads[1].wait()
    pltpu.make_async_copy(hidden, hidden, hidden_sem).wait()
    for near in range(4):
        for half in range(2):
            arrived(slot(0, 1, near, half))
    forward(0)

    order = [(0, 0), (0, 1), (1, 0), (3, 0), (1, 1), (3, 1), (2, 0), (2, 1)]
    for near, half in order:
        before, after = slot(3, 0, near, half), slot(1, 0, near, half)
        arrived(before)
        if half == 0:
            send_tokens(tokens.at[before], slot(2, 0, near, 0), far_plus)
        send_tokens(tokens.at[before], slot(3, 1, near, half), other_core)
        arrived(after)
        if half == 1:
            send_tokens(tokens.at[after], slot(2, 0, near, 1), far_minus)
        send_tokens(tokens.at[after], slot(1, 1, near, half), other_core)
    for far in (3, 1):
        for near, half in order:
            arrived(slot(far, 1, near, half))
        forward(far)
    for near, half in order:
        place = slot(2, 0, near, half)
        arrived(place)
        send_tokens(tokens.at[place], slot(2, 1, near, half), other_core)
    for near, half in order:
        arrived(slot(2, 1, near, half))
    pl.semaphore_signal(
        ready, inc=1, device_id=(above % 2, member_of(above, z, x, core)), device_id_type=BY_MESH
    )
    forward(2)
    pl.semaphore_wait(ready, 1)

    def send_sums(matrix, step):
        there_island, there = partner(step)
        number = there_island * MEMBERS + there

        @pl.when(number != me)
        def _():
            pltpu.make_async_remote_copy(
                src_ref=outgoing.at[matrix, pl.ds(number * 2, 2)],
                dst_ref=received[matrix].at[pl.ds(me * 2, 2)],
                send_sem=sums_sent,
                recv_sem=sums_got.at[matrix],
                device_id=(there_island, there),
                device_id_type=BY_MESH,
            ).start()

    def backward(matrix):
        def group_of_chips(group, carry):
            steps = [((group * 4 + k) * CHIP_STRIDE) % CHIPS for k in range(4)]
            chips = []
            for step in steps:
                there_island, there = partner(step * 2)
                chips.append(there_island * 32 + there // 2)
            columns = [
                tokens[:, :, pl.ds(pl.multiple_of(chip * BLOCK, BLOCK), BLOCK)].reshape(1024, BLOCK)
                for chip in chips
            ]
            summed = lax.dot_general(
                jnp.concatenate(columns, axis=1),
                cotangent[:, matrix * 256 : (matrix + 1) * 256],
                (((0,), (0,)), ((), ())),
                preferred_element_type=jnp.float32,
            )
            scaled = (inner_rate * summed).astype(jnp.bfloat16)
            for k in range(4):
                for half in range(2):
                    first = k * BLOCK + half * ROWS
                    for block in range(2):
                        outgoing[matrix, (chips[k] * 2 + half) * 2 + block] = scaled[
                            first : first + ROWS, block * BLOCK : (block + 1) * BLOCK
                        ]
            for k in range(4):
                send_sums(matrix, steps[k] * 2 + k % 2)
            return carry

        def other_cores(index, carry):
            send_sums(matrix, ((index * CHIP_STRIDE) % CHIPS) * 2 + (index + 1) % 2)
            return carry

        lax.fori_loop(0, CHIPS // 4, group_of_chips, 0)
        lax.fori_loop(0, CHIPS, other_cores, 0)
        received[matrix][pl.ds(me * 2, 2)] = outgoing[matrix, pl.ds(me * 2, 2)]

    backward(0)
    backward(1)
    loads[2].wait()

    mine = pl.ds(pl.multiple_of(me * ROWS, ROWS), ROWS)
    others = pl.ds(0, (PEERS - 1) * 2)
    all_others = [received[matrix].at[others] for matrix in range(2)]
    outs = (gate_out, up_out)

    def outer_step(matrix):
        def one_block(block, carry):
            first = inverse_ref[0, block]
            second = inverse_ref[1, block]
            cols = pl.ds(pl.multiple_of(block * BLOCK, BLOCK), BLOCK)
            one = received[matrix][first].astype(jnp.float32)
            two = received[matrix][second].astype(jnp.float32)
            average = (one + two) * (1.0 / ISLANDS)
            state = momentum_decay * momentum_out[matrix, :, cols].astype(jnp.float32) + average
            momentum_out[matrix, :, cols] = state.astype(jnp.bfloat16)
            update[matrix, block] = (outer_rate * (average + momentum_decay * state)).astype(
                jnp.bfloat16
            )
            return carry

        lax.fori_loop(0, PEERS, one_block, 0)

    def give_back(matrix):
        def stage(number, there_island, there):
            rows = pl.ds(pl.multiple_of(number * ROWS, ROWS), ROWS)
            for half in range(2):
                block = layout_ref[there_island, there * 2 + half]
                weights[matrix, rows, half * BLOCK : (half + 1) * BLOCK] = update[matrix, block]
            return rows

        def one_device(index, carry):
            there_island, there = partner((index * STRIDE) % PEERS)
            rows = stage(there_island * MEMBERS + there, there_island, there)
            pltpu.make_async_remote_copy(
                src_ref=weights.at[matrix, rows],
                dst_ref=outs[matrix].at[mine],
                send_sem=updates_sent,
                recv_sem=updates_got.at[matrix],
                device_id=(there_island, there),
                device_id_type=BY_MESH,
            ).start()
            return carry

        lax.fori_loop(1, PEERS, one_device, 0)
        stage(me, island, member)
        pltpu.make_async_copy(weights.at[matrix, mine], outs[matrix].at[mine], own_sem.at[matrix]).start()

    for matrix in range(2):
        pltpu.make_async_copy(all_others[matrix], all_others[matrix], sums_got.at[matrix]).wait()
        outer_step(matrix)
        give_back(matrix)

    sent = tokens.at[pl.ds(0, 63)]
    pltpu.make_async_copy(sent, sent, gather_sent).wait()
    for matrix in range(2):
        pltpu.make_async_copy(all_others[matrix], all_others[matrix], sums_sent).wait()
    for matrix in range(2):
        pltpu.make_async_copy(weights.at[matrix, mine], outs[matrix].at[mine], own_sem.at[matrix]).wait()
        part = outs[matrix].at[pl.ds(0, (PEERS - 1) * ROWS)]
        pltpu.make_async_copy(part, part, updates_got.at[matrix]).wait()
        pltpu.make_async_copy(part, part, updates_sent).wait()


def shards(tokens, hidden_grad, gate_weight, up_weight, momentum, layouts):
    blocks = layouts.shape[1]
    places = jnp.arange(blocks, dtype=jnp.int32)
    hit = layouts[:, :, None] == places[None, None, :]
    inverse = jnp.sum(jnp.where(hit, places[None, :, None], 0), axis=1, dtype=jnp.int32)
    inverse = inverse + jnp.arange(ISLANDS, dtype=jnp.int32)[:, None] * blocks
    anywhere = pl.BlockSpec(memory_space=pl.ANY)
    vmem = pl.BlockSpec(memory_space=pltpu.VMEM)
    scalars = pl.BlockSpec(memory_space=pltpu.SMEM)
    bf16 = jnp.bfloat16
    gate, up, state = pl.pallas_call(
        kernel,
        out_shape=(
            pltpu.VMEM((8192, 256), bf16),
            pltpu.VMEM((8192, 256), bf16),
            pltpu.VMEM((2, ROWS, 16384), bf16),
        ),
        in_specs=[anywhere] * 5 + [scalars] * 2,
        out_specs=(vmem, vmem, vmem),
        scratch_shapes=[
            pltpu.VMEM((MEMBERS, OWN_TOKENS, 8192), bf16),
            pltpu.VMEM((2, 8192, 256), bf16),
            pltpu.VMEM((MEMBERS, OWN_TOKENS, 256), bf16),
            pltpu.VMEM((1024, 512), bf16),
            pltpu.VMEM((2, PEERS * 2, ROWS, BLOCK), bf16),
            pltpu.VMEM((PEERS * 2, ROWS, BLOCK), bf16),
            pltpu.VMEM((PEERS * 2, ROWS, BLOCK), bf16),
            pltpu.VMEM((2, PEERS, ROWS, BLOCK), bf16),
            pltpu.VMEM((256, 256), jnp.float32),
            pltpu.VMEM((256, 256), jnp.float32),
            pltpu.SemaphoreType.DMA((3,)),
            pltpu.SemaphoreType.DMA,
            pltpu.SemaphoreType.DMA,
            pltpu.SemaphoreType.DMA,
            pltpu.SemaphoreType.DMA((64,)),
            pltpu.SemaphoreType.DMA,
            pltpu.SemaphoreType.DMA((2,)),
            pltpu.SemaphoreType.DMA((2,)),
            pltpu.SemaphoreType.DMA,
            pltpu.SemaphoreType.DMA((2,)),
            pltpu.SemaphoreType.REGULAR,
        ],
        compiler_params=pltpu.CompilerParams(
            collective_id=0, has_side_effects=True, vmem_limit_bytes=49 * 2**20
        ),
    )(tokens[0], hidden_grad[0], gate_weight[0], up_weight[0], momentum, layouts, inverse)
    return gate[None], up[None], state


def solution(mesh):
    placed = (
        P("island", "fsdp", None),
        P("island", None, "fsdp"),
        P("island", None, "fsdp"),
        P("island", None, "fsdp"),
        P(None, ("island", "fsdp"), None),
        P(),
    )
    return jax.shard_map(
        shards,
        mesh=mesh,
        in_specs=placed,
        out_specs=(
            P("island", None, "fsdp"),
            P("island", None, "fsdp"),
            P(None, ("island", "fsdp"), None),
        ),
        check_vma=False,
    )
```

```python
import jax
import jax.numpy as jnp
from jax import lax
from jax.experimental import pallas as pl
from jax.experimental.pallas import tpu as pltpu
from jax.sharding import PartitionSpec as P

BLOCK = 128
BY_MESH = pl.DeviceIdType.MESH

inner_rate = 0.25
outer_rate = 0.7
momentum_decay = 0.9

ISLANDS = 2
MEMBERS = 64
PEERS = ISLANDS * MEMBERS
CHIPS = PEERS // 2
ROWS = 64
OWN_TOKENS = 16
STRIDE = 91
CHIP_STRIDE = 29


def position():
    island = lax.axis_index("island")
    member = lax.axis_index("fsdp")
    return (member // 32) * 2 + island, (member // 8) % 4, (member // 2) % 4, member % 2


def member_of(y, z, x, core):
    return (y // 2) * 32 + z * 8 + x * 2 + core


def slot(far, sibling, near, half):
    return ((far * 2 + sibling) * 4 + near) * 2 + half


def cotangents(gate_pre, up_pre, upstream):
    logistic = jax.nn.sigmoid(gate_pre)
    d_gate = upstream * up_pre * logistic * (1.0 + gate_pre * (1.0 - logistic))
    d_up = upstream * gate_pre * logistic
    return d_gate.astype(jnp.bfloat16), d_up.astype(jnp.bfloat16)


def kernel(
    tokens_ref,
    hidden_ref,
    gate_ref,
    up_ref,
    momentum_ref,
    layout_ref,
    inverse_ref,
    gate_out,
    up_out,
    momentum_out,
    tokens,
    weights,
    hidden,
    cotangent,
    outgoing,
    gate_received,
    up_received,
    update,
    gate_sum,
    up_sum,
    load_sem,
    hidden_sem,
    tokens_sem,
    gather_sent,
    gather_got,
    sums_sent,
    sums_got,
    own_sem,
    updates_sent,
    updates_got,
    ready,
):
    received = (gate_received, up_received)
    y, z, x, core = position()
    island = lax.axis_index("island")
    member = lax.axis_index("fsdp")
    me = island * MEMBERS + member

    def partner(step):
        dy, dz, dx, dc = step // 32, (step // 8) % 4, (step // 2) % 4, step % 2
        there_y = (y + dy) % 4
        there = member_of(there_y, (z + dz) % 4, (x + dx) % 4, (core + dc) % 2)
        return there_y % 2, there

    near_plus, near_minus, far_plus, far_minus = (
        member_of(y, (z + dz) % 4, (x + dx) % 4, core)
        for dz, dx in (
            (core, 1 - core),
            (3 * core, 3 * (1 - core)),
            (1 - core, core),
            (3 * (1 - core), 3 * core),
        )
    )
    other_plane = member_of((y + 2) % 4, z, x, core)
    other_core = member_of(y, z, x, 1 - core)
    above, below = (y + 1) % 4, (y + 3) % 4
    barrier = pltpu.get_barrier_semaphore()
    greeted = [(island, near_plus), (island, near_minus), (island, far_plus), (island, far_minus)]
    greeted += [(island, other_plane), (island, other_core)]
    greeted += [(below % 2, member_of(below, z, x, core))]
    for there in greeted:
        pl.semaphore_signal(barrier, inc=1, device_id=there, device_id_type=BY_MESH)

    loads = [
        pltpu.make_async_copy(gate_ref, weights.at[0], load_sem.at[0]),
        pltpu.make_async_copy(up_ref, weights.at[1], load_sem.at[1]),
        pltpu.make_async_copy(momentum_ref, momentum_out, load_sem.at[2]),
    ]
    own_tokens = pltpu.make_async_copy(tokens_ref, tokens.at[0], tokens_sem)
    own_tokens.start()

    def load_hidden(place, carry):
        half, near, sibling, far = place % 2, (place // 2) % 4, (place // 8) % 2, place // 16
        their_core = (core + sibling) % 2
        dx = near * (1 - their_core) + far * their_core
        dz = near * their_core + far * (1 - their_core)
        there = member_of((y + 2 * half) % 4, (z + dz) % 4, (x + dx) % 4, their_core)
        rows = pl.ds(pl.multiple_of(there * OWN_TOKENS, OWN_TOKENS), OWN_TOKENS)
        pltpu.make_async_copy(hidden_ref.at[rows], hidden.at[place], hidden_sem).start()
        return carry

    lax.fori_loop(0, MEMBERS, load_hidden, 0)
    for load in loads:
        load.start()

    pl.semaphore_wait(barrier, len(greeted))

    def send_tokens(source, place, part, to):
        cols = pl.ds(part * 4096, 4096)
        pltpu.make_async_remote_copy(
            src_ref=source.at[:, cols],
            dst_ref=tokens.at[place, :, cols],
            send_sem=gather_sent,
            recv_sem=gather_got.at[place * 2 + part],
            device_id=(island, to),
            device_id_type=BY_MESH,
        ).start()

    def arrived(place, part):
        block = tokens.at[place, :, pl.ds(part * 4096, 4096)]
        pltpu.make_async_copy(block, block, gather_got.at[place * 2 + part]).wait()

    parts = range(2)

    def spread(source, near, half, part):
        send_tokens(source, slot(3, 0, near, half), part, far_plus)
        send_tokens(source, slot(1, 0, near, half), part, far_minus)
        send_tokens(source, slot(0, 1, near, half), part, other_core)

    def ring(source, half, part):
        send_tokens(source, slot(0, 0, 3, half), part, near_plus)
        send_tokens(source, slot(0, 0, 1, half), part, near_minus)

    for part in parts:
        send_tokens(tokens_ref, slot(0, 0, 0, 1), part, other_plane)
        ring(tokens_ref, 0, part)
        spread(tokens_ref, 0, 0, part)

    before, after = slot(0, 0, 3, 0), slot(0, 0, 1, 0)
    for part in parts:
        arrived(before, part)
        send_tokens(tokens.at[before], slot(0, 0, 3, 1), part, other_plane)
        if part % 2 == 0:
            send_tokens(tokens.at[before], slot(0, 0, 2, 0), part, near_plus)
        arrived(after, part)
        send_tokens(tokens.at[after], slot(0, 0, 1, 1), part, other_plane)
        if part % 2 == 1:
            send_tokens(tokens.at[after], slot(0, 0, 2, 0), part, near_minus)
        spread(tokens.at[before], 3, 0, part)
        spread(tokens.at[after], 1, 0, part)
    for part in parts:
        arrived(slot(0, 0, 0, 1), part)
        spread(tokens.at[slot(0, 0, 0, 1)], 0, 1, part)
    place = slot(0, 0, 2, 0)
    for part in parts:
        arrived(place, part)
        send_tokens(tokens.at[place], slot(0, 0, 2, 1), part, other_plane)
        spread(tokens.at[place], 2, 0, part)
    for near in (3, 1, 2):
        place = slot(0, 0, near, 1)
        for part in parts:
            arrived(place, part)
            spread(tokens.at[place], near, 1, part)

    def forward(far):
        depth = 1024
        for part in range(8):
            cols = pl.ds(part * depth, depth)
            rows = tokens[pl.ds(far * 16, 16), :, cols].reshape(256, depth)
            gate_part = jnp.dot(rows, weights[0, cols, :], preferred_element_type=jnp.float32)
            up_part = jnp.dot(rows, weights[1, cols, :], preferred_element_type=jnp.float32)
            if part == 0:
                gate_sum[...] = gate_part
                up_sum[...] = up_part
            else:
                gate_sum[...] += gate_part
                up_sum[...] += up_part
        upstream = hidden[pl.ds(far * 16, 16)].reshape(256, 256).astype(jnp.float32)
        d_gate, d_up = cotangents(gate_sum[...], up_sum[...], upstream)
        cotangent[pl.ds(far * 256, 256), 0:256] = d_gate
        cotangent[pl.ds(far * 256, 256), 256:512] = d_up

    own_tokens.wait()
    loads[0].wait()
    loads[1].wait()
    pltpu.make_async_copy(hidden, hidden, hidden_sem).wait()
    def all_from_other_core(far):
        for near in range(4):
            for half in range(2):
                for part in parts:
                    arrived(slot(far, 1, near, half), part)

    all_from_other_core(0)
    forward(0)
    order = [(0, 0), (0, 1), (1, 0), (3, 0), (1, 1), (3, 1), (2, 0), (2, 1)]
    for near, half in order:
        before, after = slot(3, 0, near, half), slot(1, 0, near, half)
        for part in parts:
            arrived(before, part)
            if half == 0:
                send_tokens(tokens.at[before], slot(2, 0, near, 0), part, far_plus)
            send_tokens(tokens.at[before], slot(3, 1, near, half), part, other_core)
            arrived(after, part)
            if half == 1:
                send_tokens(tokens.at[after], slot(2, 0, near, 1), part, far_minus)
            send_tokens(tokens.at[after], slot(1, 1, near, half), part, other_core)
    for far in (3, 1):
        all_from_other_core(far)
        forward(far)
    for near, half in order:
        place = slot(2, 0, near, half)
        for part in parts:
            arrived(place, part)
            send_tokens(tokens.at[place], slot(2, 1, near, half), part, other_core)
    all_from_other_core(2)
    pl.semaphore_signal(
        ready, inc=1, device_id=(above % 2, member_of(above, z, x, core)), device_id_type=BY_MESH
    )
    forward(2)
    pl.semaphore_wait(ready, 1)

    def send_sums(matrix, step):
        there_island, there = partner(step)
        number = there_island * MEMBERS + there

        @pl.when(number != me)
        def _():
            pltpu.make_async_remote_copy(
                src_ref=outgoing.at[matrix, pl.ds(number * 2, 2)],
                dst_ref=received[matrix].at[pl.ds(me * 2, 2)],
                send_sem=sums_sent,
                recv_sem=sums_got.at[matrix],
                device_id=(there_island, there),
                device_id_type=BY_MESH,
            ).start()

    def backward(matrix):
        def group_of_chips(group, carry):
            steps = [((group * 4 + k) * CHIP_STRIDE) % CHIPS for k in range(4)]
            chips = []
            for step in steps:
                there_island, there = partner(step * 2)
                chips.append(there_island * 32 + there // 2)
            columns = [
                tokens[:, :, pl.ds(pl.multiple_of(chip * BLOCK, BLOCK), BLOCK)].reshape(1024, BLOCK)
                for chip in chips
            ]
            summed = lax.dot_general(
                jnp.concatenate(columns, axis=1),
                cotangent[:, matrix * 256 : (matrix + 1) * 256],
                (((0,), (0,)), ((), ())),
                preferred_element_type=jnp.float32,
            )
            scaled = (inner_rate * summed).astype(jnp.bfloat16)
            for k in range(4):
                for half in range(2):
                    first = k * BLOCK + half * ROWS
                    for block in range(2):
                        outgoing[matrix, (chips[k] * 2 + half) * 2 + block] = scaled[
                            first : first + ROWS, block * BLOCK : (block + 1) * BLOCK
                        ]
            for k in range(4):
                send_sums(matrix, steps[k] * 2 + k % 2)
            return carry

        def other_cores(index, carry):
            send_sums(matrix, ((index * CHIP_STRIDE) % CHIPS) * 2 + (index + 1) % 2)
            return carry

        lax.fori_loop(0, CHIPS // 4, group_of_chips, 0)
        lax.fori_loop(0, CHIPS, other_cores, 0)
        received[matrix][pl.ds(me * 2, 2)] = outgoing[matrix, pl.ds(me * 2, 2)]

    backward(0)
    backward(1)
    loads[2].wait()

    mine = pl.ds(pl.multiple_of(me * ROWS, ROWS), ROWS)
    others = pl.ds(0, (PEERS - 1) * 2)
    all_others = [received[matrix].at[others] for matrix in range(2)]
    outs = (gate_out, up_out)

    def outer_step(matrix):
        def one_block(block, carry):
            first = inverse_ref[0, block]
            second = inverse_ref[1, block]
            cols = pl.ds(pl.multiple_of(block * BLOCK, BLOCK), BLOCK)
            one = received[matrix][first].astype(jnp.float32)
            two = received[matrix][second].astype(jnp.float32)
            average = (one + two) * (1.0 / ISLANDS)
            state = momentum_decay * momentum_out[matrix, :, cols].astype(jnp.float32) + average
            momentum_out[matrix, :, cols] = state.astype(jnp.bfloat16)
            update[matrix, block] = (outer_rate * (average + momentum_decay * state)).astype(
                jnp.bfloat16
            )
            return carry

        lax.fori_loop(0, PEERS, one_block, 0)

    def give_back(matrix):
        def stage(number, there_island, there):
            rows = pl.ds(pl.multiple_of(number * ROWS, ROWS), ROWS)
            for half in range(2):
                block = layout_ref[there_island, there * 2 + half]
                weights[matrix, rows, half * BLOCK : (half + 1) * BLOCK] = update[matrix, block]
            return rows

        def one_device(index, carry):
            there_island, there = partner((index * STRIDE) % PEERS)
            rows = stage(there_island * MEMBERS + there, there_island, there)
            pltpu.make_async_remote_copy(
                src_ref=weights.at[matrix, rows],
                dst_ref=outs[matrix].at[mine],
                send_sem=updates_sent,
                recv_sem=updates_got.at[matrix],
                device_id=(there_island, there),
                device_id_type=BY_MESH,
            ).start()
            return carry

        lax.fori_loop(1, PEERS, one_device, 0)
        stage(me, island, member)
        pltpu.make_async_copy(weights.at[matrix, mine], outs[matrix].at[mine], own_sem.at[matrix]).start()

    for matrix in range(2):
        pltpu.make_async_copy(all_others[matrix], all_others[matrix], sums_got.at[matrix]).wait()
        outer_step(matrix)
        give_back(matrix)

    sent = tokens.at[pl.ds(0, 63)]
    pltpu.make_async_copy(sent, sent, gather_sent).wait()
    for matrix in range(2):
        pltpu.make_async_copy(all_others[matrix], all_others[matrix], sums_sent).wait()
    for matrix in range(2):
        pltpu.make_async_copy(weights.at[matrix, mine], outs[matrix].at[mine], own_sem.at[matrix]).wait()
        part = outs[matrix].at[pl.ds(0, (PEERS - 1) * ROWS)]
        pltpu.make_async_copy(part, part, updates_got.at[matrix]).wait()
        pltpu.make_async_copy(part, part, updates_sent).wait()


def shards(tokens, hidden_grad, gate_weight, up_weight, momentum, layouts):
    blocks = layouts.shape[1]
    places = jnp.arange(blocks, dtype=jnp.int32)
    hit = layouts[:, :, None] == places[None, None, :]
    lies = jnp.arange(ISLANDS * blocks, dtype=jnp.int32).reshape(ISLANDS, blocks)
    inverse = jnp.sum(jnp.where(hit, lies[:, :, None], 0), axis=1, dtype=jnp.int32)
    anywhere = pl.BlockSpec(memory_space=pl.ANY)
    vmem = pl.BlockSpec(memory_space=pltpu.VMEM)
    scalars = pl.BlockSpec(memory_space=pltpu.SMEM)
    bf16 = jnp.bfloat16
    gate, up, state = pl.pallas_call(
        kernel,
        out_shape=(
            pltpu.VMEM((8192, 256), bf16),
            pltpu.VMEM((8192, 256), bf16),
            pltpu.VMEM((2, ROWS, 16384), bf16),
        ),
        in_specs=[anywhere] * 5 + [scalars] * 2,
        out_specs=(vmem, vmem, vmem),
        scratch_shapes=[
            pltpu.VMEM((MEMBERS, OWN_TOKENS, 8192), bf16),
            pltpu.VMEM((2, 8192, 256), bf16),
            pltpu.VMEM((MEMBERS, OWN_TOKENS, 256), bf16),
            pltpu.VMEM((1024, 512), bf16),
            pltpu.VMEM((2, PEERS * 2, ROWS, BLOCK), bf16),
            pltpu.VMEM((PEERS * 2, ROWS, BLOCK), bf16),
            pltpu.VMEM((PEERS * 2, ROWS, BLOCK), bf16),
            pltpu.VMEM((2, PEERS, ROWS, BLOCK), bf16),
            pltpu.VMEM((256, 256), jnp.float32),
            pltpu.VMEM((256, 256), jnp.float32),
            pltpu.SemaphoreType.DMA((3,)),
            pltpu.SemaphoreType.DMA,
            pltpu.SemaphoreType.DMA,
            pltpu.SemaphoreType.DMA,
            pltpu.SemaphoreType.DMA((128,)),
            pltpu.SemaphoreType.DMA,
            pltpu.SemaphoreType.DMA((2,)),
            pltpu.SemaphoreType.DMA((2,)),
            pltpu.SemaphoreType.DMA,
            pltpu.SemaphoreType.DMA((2,)),
            pltpu.SemaphoreType.REGULAR,
        ],
        compiler_params=pltpu.CompilerParams(
            collective_id=0, has_side_effects=True, vmem_limit_bytes=49 * 2**20
        ),
    )(tokens[0], hidden_grad[0], gate_weight[0], up_weight[0], momentum, layouts, inverse)
    return gate[None], up[None], state


def solution(mesh):
    placed = (
        P("island", "fsdp", None),
        P("island", None, "fsdp"),
        P("island", None, "fsdp"),
        P("island", None, "fsdp"),
        P(None, ("island", "fsdp"), None),
        P(),
    )
    return jax.shard_map(
        shards,
        mesh=mesh,
        in_specs=placed,
        out_specs=(
            P("island", None, "fsdp"),
            P("island", None, "fsdp"),
            P(None, ("island", "fsdp"), None),
        ),
        check_vma=False,
    )
```

```python
import jax
import jax.numpy as jnp
from jax import lax
from jax.experimental import pallas as pl
from jax.experimental.pallas import tpu as pltpu
from jax.sharding import PartitionSpec as P

BLOCK = 128
BY_MESH = pl.DeviceIdType.MESH

inner_rate = 0.25
outer_rate = 0.7
momentum_decay = 0.9

ISLANDS = 2
MEMBERS = 64
PEERS = ISLANDS * MEMBERS
CHIPS = PEERS // 2
ROWS = 64
OWN_TOKENS = 16
STRIDE = 59
CHIP_STRIDE = 29


def position():
    island = lax.axis_index("island")
    member = lax.axis_index("fsdp")
    return (member // 32) * 2 + island, (member // 8) % 4, (member // 2) % 4, member % 2


def member_of(y, z, x, core):
    return (y // 2) * 32 + z * 8 + x * 2 + core


def slot(far, sibling, near, half):
    return ((far * 2 + sibling) * 4 + near) * 2 + half


def cotangents(gate_pre, up_pre, upstream):
    logistic = jax.nn.sigmoid(gate_pre)
    d_gate = upstream * up_pre * logistic * (1.0 + gate_pre * (1.0 - logistic))
    d_up = upstream * gate_pre * logistic
    return d_gate.astype(jnp.bfloat16), d_up.astype(jnp.bfloat16)


def kernel(
    tokens_ref,
    hidden_ref,
    gate_ref,
    up_ref,
    momentum_ref,
    layout_ref,
    inverse_ref,
    gate_out,
    up_out,
    momentum_out,
    tokens,
    weights,
    hidden,
    cotangent,
    outgoing,
    gate_received,
    up_received,
    update,
    gate_sum,
    up_sum,
    load_sem,
    hidden_sem,
    tokens_sem,
    gather_sent,
    gather_got,
    sums_sent,
    sums_got,
    own_sem,
    updates_sent,
    updates_got,
    ready,
):
    received = (gate_received, up_received)
    y, z, x, core = position()
    island = lax.axis_index("island")
    member = lax.axis_index("fsdp")
    me = island * MEMBERS + member

    def partner(step):
        first, second, third, dc = step // 32, (step // 8) % 4, (step // 2) % 4, step % 2
        dy = first * (1 - core) + second * core
        dz = second * (1 - core) + third * core
        dx = third * (1 - core) + first * core
        there_y = (y + dy) % 4
        there = member_of(there_y, (z + dz) % 4, (x + dx) % 4, (core + dc) % 2)
        return there_y % 2, there

    near_plus, near_minus, far_plus, far_minus = (
        member_of(y, (z + dz) % 4, (x + dx) % 4, core)
        for dz, dx in (
            (core, 1 - core),
            (3 * core, 3 * (1 - core)),
            (1 - core, core),
            (3 * (1 - core), 3 * core),
        )
    )
    other_plane = member_of((y + 2) % 4, z, x, core)
    other_core = member_of(y, z, x, 1 - core)
    above, below = (y + 1) % 4, (y + 3) % 4
    barrier = pltpu.get_barrier_semaphore()
    greeted = [(island, near_plus), (island, near_minus), (island, far_plus), (island, far_minus)]
    greeted += [(island, other_plane), (island, other_core)]
    greeted += [(below % 2, member_of(below, z, x, core))]
    for there in greeted:
        pl.semaphore_signal(barrier, inc=1, device_id=there, device_id_type=BY_MESH)

    loads = [
        pltpu.make_async_copy(gate_ref, weights.at[0], load_sem.at[0]),
        pltpu.make_async_copy(up_ref, weights.at[1], load_sem.at[1]),
        pltpu.make_async_copy(momentum_ref, momentum_out, load_sem.at[2]),
    ]
    own_tokens = pltpu.make_async_copy(tokens_ref, tokens.at[0], tokens_sem)
    own_tokens.start()

    def load_hidden(place, carry):
        half, near, sibling, far = place % 2, (place // 2) % 4, (place // 8) % 2, place // 16
        their_core = (core + sibling) % 2
        dx = near * (1 - their_core) + far * their_core
        dz = near * their_core + far * (1 - their_core)
        there = member_of((y + 2 * half) % 4, (z + dz) % 4, (x + dx) % 4, their_core)
        rows = pl.ds(pl.multiple_of(there * OWN_TOKENS, OWN_TOKENS), OWN_TOKENS)
        pltpu.make_async_copy(hidden_ref.at[rows], hidden.at[place], hidden_sem).start()
        return carry

    lax.fori_loop(0, MEMBERS, load_hidden, 0)
    for load in loads:
        load.start()

    pl.semaphore_wait(barrier, len(greeted))

    def send_tokens(source, place, part, to):
        cols = pl.ds(part * 4096, 4096)
        pltpu.make_async_remote_copy(
            src_ref=source.at[:, cols],
            dst_ref=tokens.at[place, :, cols],
            send_sem=gather_sent,
            recv_sem=gather_got.at[place * 2 + part],
            device_id=(island, to),
            device_id_type=BY_MESH,
        ).start()

    def arrived(place, part):
        block = tokens.at[place, :, pl.ds(part * 4096, 4096)]
        pltpu.make_async_copy(block, block, gather_got.at[place * 2 + part]).wait()

    parts = range(2)

    def spread(source, near, half, part):
        send_tokens(source, slot(3, 0, near, half), part, far_plus)
        send_tokens(source, slot(1, 0, near, half), part, far_minus)
        send_tokens(source, slot(0, 1, near, half), part, other_core)

    def ring(source, half, part):
        send_tokens(source, slot(0, 0, 3, half), part, near_plus)
        send_tokens(source, slot(0, 0, 1, half), part, near_minus)

    for part in parts:
        send_tokens(tokens_ref, slot(0, 0, 0, 1), part, other_plane)
        ring(tokens_ref, 0, part)
        spread(tokens_ref, 0, 0, part)

    before, after = slot(0, 0, 3, 0), slot(0, 0, 1, 0)
    for part in parts:
        arrived(before, part)
        send_tokens(tokens.at[before], slot(0, 0, 3, 1), part, other_plane)
        if part % 2 == 0:
            send_tokens(tokens.at[before], slot(0, 0, 2, 0), part, near_plus)
        arrived(after, part)
        send_tokens(tokens.at[after], slot(0, 0, 1, 1), part, other_plane)
        if part % 2 == 1:
            send_tokens(tokens.at[after], slot(0, 0, 2, 0), part, near_minus)
        spread(tokens.at[before], 3, 0, part)
        spread(tokens.at[after], 1, 0, part)
    for part in parts:
        arrived(slot(0, 0, 0, 1), part)
        spread(tokens.at[slot(0, 0, 0, 1)], 0, 1, part)
    place = slot(0, 0, 2, 0)
    for part in parts:
        arrived(place, part)
        send_tokens(tokens.at[place], slot(0, 0, 2, 1), part, other_plane)
        spread(tokens.at[place], 2, 0, part)
    for near in (3, 1, 2):
        place = slot(0, 0, near, 1)
        for part in parts:
            arrived(place, part)
            spread(tokens.at[place], near, 1, part)

    def forward(far):
        depth = 1024
        for part in range(8):
            cols = pl.ds(part * depth, depth)
            rows = tokens[pl.ds(far * 16, 16), :, cols].reshape(256, depth)
            gate_part = jnp.dot(rows, weights[0, cols, :], preferred_element_type=jnp.float32)
            up_part = jnp.dot(rows, weights[1, cols, :], preferred_element_type=jnp.float32)
            if part == 0:
                gate_sum[...] = gate_part
                up_sum[...] = up_part
            else:
                gate_sum[...] += gate_part
                up_sum[...] += up_part
        upstream = hidden[pl.ds(far * 16, 16)].reshape(256, 256).astype(jnp.float32)
        d_gate, d_up = cotangents(gate_sum[...], up_sum[...], upstream)
        cotangent[pl.ds(far * 256, 256), 0:256] = d_gate
        cotangent[pl.ds(far * 256, 256), 256:512] = d_up

    own_tokens.wait()
    loads[0].wait()
    loads[1].wait()
    pltpu.make_async_copy(hidden, hidden, hidden_sem).wait()
    def all_from_other_core(far):
        for near in range(4):
            for half in range(2):
                for part in parts:
                    arrived(slot(far, 1, near, half), part)

    all_from_other_core(0)
    forward(0)
    order = [(0, 0), (0, 1), (1, 0), (3, 0), (1, 1), (3, 1), (2, 0), (2, 1)]
    for near, half in order:
        before, after = slot(3, 0, near, half), slot(1, 0, near, half)
        for part in parts:
            arrived(before, part)
            if half == 0:
                send_tokens(tokens.at[before], slot(2, 0, near, 0), part, far_plus)
            send_tokens(tokens.at[before], slot(3, 1, near, half), part, other_core)
            arrived(after, part)
            if half == 1:
                send_tokens(tokens.at[after], slot(2, 0, near, 1), part, far_minus)
            send_tokens(tokens.at[after], slot(1, 1, near, half), part, other_core)
    for far in (3, 1):
        all_from_other_core(far)
        forward(far)
    for near, half in order:
        place = slot(2, 0, near, half)
        for part in parts:
            arrived(place, part)
            send_tokens(tokens.at[place], slot(2, 1, near, half), part, other_core)
    all_from_other_core(2)
    pl.semaphore_signal(
        ready, inc=1, device_id=(above % 2, member_of(above, z, x, core)), device_id_type=BY_MESH
    )
    forward(2)
    pl.semaphore_wait(ready, 1)

    def send_sums(matrix, step):
        there_island, there = partner(step)
        number = there_island * MEMBERS + there

        @pl.when(number != me)
        def _():
            pltpu.make_async_remote_copy(
                src_ref=outgoing.at[matrix, pl.ds(number * 2, 2)],
                dst_ref=received[matrix].at[pl.ds(me * 2, 2)],
                send_sem=sums_sent,
                recv_sem=sums_got.at[matrix],
                device_id=(there_island, there),
                device_id_type=BY_MESH,
            ).start()

    def backward(matrix):
        def group_of_chips(group, carry):
            steps = [((group * 4 + k) * CHIP_STRIDE) % CHIPS for k in range(4)]
            chips = []
            for step in steps:
                there_island, there = partner(step * 2)
                chips.append(there_island * 32 + there // 2)
            columns = [
                tokens[:, :, pl.ds(pl.multiple_of(chip * BLOCK, BLOCK), BLOCK)].reshape(1024, BLOCK)
                for chip in chips
            ]
            summed = lax.dot_general(
                jnp.concatenate(columns, axis=1),
                cotangent[:, matrix * 256 : (matrix + 1) * 256],
                (((0,), (0,)), ((), ())),
                preferred_element_type=jnp.float32,
            )
            scaled = (inner_rate * summed).astype(jnp.bfloat16)
            for k in range(4):
                for half in range(2):
                    first = k * BLOCK + half * ROWS
                    for block in range(2):
                        outgoing[matrix, (chips[k] * 2 + half) * 2 + block] = scaled[
                            first : first + ROWS, block * BLOCK : (block + 1) * BLOCK
                        ]
            for k in range(4):
                send_sums(matrix, steps[k] * 2 + k % 2)
            return carry

        def other_cores(index, carry):
            send_sums(matrix, ((index * CHIP_STRIDE) % CHIPS) * 2 + (index + 1) % 2)
            return carry

        lax.fori_loop(0, CHIPS // 4, group_of_chips, 0)
        lax.fori_loop(0, CHIPS, other_cores, 0)
        received[matrix][pl.ds(me * 2, 2)] = outgoing[matrix, pl.ds(me * 2, 2)]

    backward(0)
    backward(1)
    loads[2].wait()

    mine = pl.ds(pl.multiple_of(me * ROWS, ROWS), ROWS)
    others = pl.ds(0, (PEERS - 1) * 2)
    all_others = [received[matrix].at[others] for matrix in range(2)]
    outs = (gate_out, up_out)

    def outer_step(matrix):
        def one_block(block, carry):
            first = inverse_ref[0, block]
            second = inverse_ref[1, block]
            cols = pl.ds(pl.multiple_of(block * BLOCK, BLOCK), BLOCK)
            one = received[matrix][first].astype(jnp.float32)
            two = received[matrix][second].astype(jnp.float32)
            average = (one + two) * (1.0 / ISLANDS)
            state = momentum_decay * momentum_out[matrix, :, cols].astype(jnp.float32) + average
            momentum_out[matrix, :, cols] = state.astype(jnp.bfloat16)
            update[matrix, block] = (outer_rate * (average + momentum_decay * state)).astype(
                jnp.bfloat16
            )
            return carry

        lax.fori_loop(0, PEERS, one_block, 0)

    def give_back(matrix):
        def stage(number, there_island, there):
            rows = pl.ds(pl.multiple_of(number * ROWS, ROWS), ROWS)
            for half in range(2):
                block = layout_ref[there_island, there * 2 + half]
                weights[matrix, rows, half * BLOCK : (half + 1) * BLOCK] = update[matrix, block]
            return rows

        def one_device(index, carry):
            there_island, there = partner((index * STRIDE) % PEERS)
            rows = stage(there_island * MEMBERS + there, there_island, there)
            pltpu.make_async_remote_copy(
                src_ref=weights.at[matrix, rows],
                dst_ref=outs[matrix].at[mine],
                send_sem=updates_sent,
                recv_sem=updates_got.at[matrix],
                device_id=(there_island, there),
                device_id_type=BY_MESH,
            ).start()
            return carry

        lax.fori_loop(1, PEERS, one_device, 0)
        stage(me, island, member)
        pltpu.make_async_copy(weights.at[matrix, mine], outs[matrix].at[mine], own_sem.at[matrix]).start()

    for matrix in range(2):
        pltpu.make_async_copy(all_others[matrix], all_others[matrix], sums_got.at[matrix]).wait()
        outer_step(matrix)
        give_back(matrix)

    sent = tokens.at[pl.ds(0, 63)]
    pltpu.make_async_copy(sent, sent, gather_sent).wait()
    for matrix in range(2):
        pltpu.make_async_copy(all_others[matrix], all_others[matrix], sums_sent).wait()
    for matrix in range(2):
        pltpu.make_async_copy(weights.at[matrix, mine], outs[matrix].at[mine], own_sem.at[matrix]).wait()
        part = outs[matrix].at[pl.ds(0, (PEERS - 1) * ROWS)]
        pltpu.make_async_copy(part, part, updates_got.at[matrix]).wait()
        pltpu.make_async_copy(part, part, updates_sent).wait()


def shards(tokens, hidden_grad, gate_weight, up_weight, momentum, layouts):
    blocks = layouts.shape[1]
    places = jnp.arange(blocks, dtype=jnp.int32)
    hit = layouts[:, :, None] == places[None, None, :]
    lies = jnp.arange(ISLANDS * blocks, dtype=jnp.int32).reshape(ISLANDS, blocks)
    inverse = jnp.sum(jnp.where(hit, lies[:, :, None], 0), axis=1, dtype=jnp.int32)
    anywhere = pl.BlockSpec(memory_space=pl.ANY)
    vmem = pl.BlockSpec(memory_space=pltpu.VMEM)
    scalars = pl.BlockSpec(memory_space=pltpu.SMEM)
    bf16 = jnp.bfloat16
    gate, up, state = pl.pallas_call(
        kernel,
        out_shape=(
            pltpu.VMEM((8192, 256), bf16),
            pltpu.VMEM((8192, 256), bf16),
            pltpu.VMEM((2, ROWS, 16384), bf16),
        ),
        in_specs=[anywhere] * 5 + [scalars] * 2,
        out_specs=(vmem, vmem, vmem),
        scratch_shapes=[
            pltpu.VMEM((MEMBERS, OWN_TOKENS, 8192), bf16),
            pltpu.VMEM((2, 8192, 256), bf16),
            pltpu.VMEM((MEMBERS, OWN_TOKENS, 256), bf16),
            pltpu.VMEM((1024, 512), bf16),
            pltpu.VMEM((2, PEERS * 2, ROWS, BLOCK), bf16),
            pltpu.VMEM((PEERS * 2, ROWS, BLOCK), bf16),
            pltpu.VMEM((PEERS * 2, ROWS, BLOCK), bf16),
            pltpu.VMEM((2, PEERS, ROWS, BLOCK), bf16),
            pltpu.VMEM((256, 256), jnp.float32),
            pltpu.VMEM((256, 256), jnp.float32),
            pltpu.SemaphoreType.DMA((3,)),
            pltpu.SemaphoreType.DMA,
            pltpu.SemaphoreType.DMA,
            pltpu.SemaphoreType.DMA,
            pltpu.SemaphoreType.DMA((128,)),
            pltpu.SemaphoreType.DMA,
            pltpu.SemaphoreType.DMA((2,)),
            pltpu.SemaphoreType.DMA((2,)),
            pltpu.SemaphoreType.DMA,
            pltpu.SemaphoreType.DMA((2,)),
            pltpu.SemaphoreType.REGULAR,
        ],
        compiler_params=pltpu.CompilerParams(
            collective_id=0, has_side_effects=True, vmem_limit_bytes=49 * 2**20
        ),
    )(tokens[0], hidden_grad[0], gate_weight[0], up_weight[0], momentum, layouts, inverse)
    return gate[None], up[None], state


def solution(mesh):
    placed = (
        P("island", "fsdp", None),
        P("island", None, "fsdp"),
        P("island", None, "fsdp"),
        P("island", None, "fsdp"),
        P(None, ("island", "fsdp"), None),
        P(),
    )
    return jax.shard_map(
        shards,
        mesh=mesh,
        in_specs=placed,
        out_specs=(
            P("island", None, "fsdp"),
            P("island", None, "fsdp"),
            P(None, ("island", "fsdp"), None),
        ),
        check_vma=False,
    )
```

```python
import jax
import jax.numpy as jnp
from jax import lax
from jax.experimental import pallas as pl
from jax.experimental.pallas import tpu as pltpu
from jax.sharding import PartitionSpec as P

BLOCK = 128
BY_MESH = pl.DeviceIdType.MESH

inner_rate = 0.25
outer_rate = 0.7
momentum_decay = 0.9

ISLANDS = 2
MEMBERS = 64
PEERS = ISLANDS * MEMBERS
CHIPS = PEERS // 2
ROWS = 64
OWN_TOKENS = 16
STRIDE = 59
CHIP_STRIDE = 29


def position():
    island = lax.axis_index("island")
    member = lax.axis_index("fsdp")
    return (member // 32) * 2 + island, (member // 8) % 4, (member // 2) % 4, member % 2


def member_of(y, z, x, core):
    return (y // 2) * 32 + z * 8 + x * 2 + core


def slot(far, sibling, near, half):
    return ((far * 2 + sibling) * 4 + near) * 2 + half


def cotangents(gate_pre, up_pre, upstream):
    logistic = jax.nn.sigmoid(gate_pre)
    d_gate = upstream * up_pre * logistic * (1.0 + gate_pre * (1.0 - logistic))
    d_up = upstream * gate_pre * logistic
    return d_gate.astype(jnp.bfloat16), d_up.astype(jnp.bfloat16)


def kernel(
    tokens_ref,
    hidden_ref,
    gate_ref,
    up_ref,
    momentum_ref,
    layout_ref,
    inverse_ref,
    gate_out,
    up_out,
    momentum_out,
    tokens,
    weights,
    hidden,
    cotangent,
    outgoing,
    gate_received,
    up_received,
    update,
    gate_sum,
    up_sum,
    load_sem,
    hidden_sem,
    tokens_sem,
    gather_sent,
    gather_got,
    sums_sent,
    sums_got,
    own_sem,
    updates_sent,
    updates_got,
    ready,
):
    received = (gate_received, up_received)
    y, z, x, core = position()
    island = lax.axis_index("island")
    member = lax.axis_index("fsdp")
    me = island * MEMBERS + member

    def partner(step):
        first, second, third, dc = step // 32, (step // 8) % 4, (step // 2) % 4, step % 2
        dy = first * (1 - core) + second * core
        dz = second * (1 - core) + third * core
        dx = third * (1 - core) + first * core
        there_y = (y + dy) % 4
        there = member_of(there_y, (z + dz) % 4, (x + dx) % 4, (core + dc) % 2)
        return there_y % 2, there

    near_plus, near_minus, far_plus, far_minus = (
        member_of(y, (z + dz) % 4, (x + dx) % 4, core)
        for dz, dx in (
            (core, 1 - core),
            (3 * core, 3 * (1 - core)),
            (1 - core, core),
            (3 * (1 - core), 3 * core),
        )
    )
    other_plane = member_of((y + 2) % 4, z, x, core)
    other_core = member_of(y, z, x, 1 - core)
    above, below = (y + 1) % 4, (y + 3) % 4
    barrier = pltpu.get_barrier_semaphore()
    greeted = [(island, near_plus), (island, near_minus), (island, far_plus), (island, far_minus)]
    greeted += [(island, other_plane), (island, other_core)]
    greeted += [(below % 2, member_of(below, z, x, core))]
    for there in greeted:
        pl.semaphore_signal(barrier, inc=1, device_id=there, device_id_type=BY_MESH)

    loads = [
        pltpu.make_async_copy(gate_ref, weights.at[0], load_sem.at[0]),
        pltpu.make_async_copy(up_ref, weights.at[1], load_sem.at[1]),
        pltpu.make_async_copy(momentum_ref, momentum_out, load_sem.at[2]),
    ]
    own_tokens = pltpu.make_async_copy(tokens_ref, tokens.at[0], tokens_sem)
    own_tokens.start()

    pl.semaphore_wait(barrier, len(greeted))

    def send_tokens(source, place, part, to):
        cols = pl.ds(part * 4096, 4096)
        pltpu.make_async_remote_copy(
            src_ref=source.at[:, cols],
            dst_ref=tokens.at[place, :, cols],
            send_sem=gather_sent,
            recv_sem=gather_got.at[place * 2 + part],
            device_id=(island, to),
            device_id_type=BY_MESH,
        ).start()

    def arrived(place, part):
        block = tokens.at[place, :, pl.ds(part * 4096, 4096)]
        pltpu.make_async_copy(block, block, gather_got.at[place * 2 + part]).wait()

    parts = range(2)

    def spread(source, near, half, part):
        send_tokens(source, slot(3, 0, near, half), part, far_plus)
        send_tokens(source, slot(1, 0, near, half), part, far_minus)
        send_tokens(source, slot(0, 1, near, half), part, other_core)

    def ring(source, half, part):
        send_tokens(source, slot(0, 0, 3, half), part, near_plus)
        send_tokens(source, slot(0, 0, 1, half), part, near_minus)

    for part in parts:
        send_tokens(tokens_ref, slot(0, 0, 0, 1), part, other_plane)
        ring(tokens_ref, 0, part)
        spread(tokens_ref, 0, 0, part)

    for load in loads:
        load.start()

    def load_hidden(place, carry):
        half, near, sibling, far = place % 2, (place // 2) % 4, (place // 8) % 2, place // 16
        their_core = (core + sibling) % 2
        dx = near * (1 - their_core) + far * their_core
        dz = near * their_core + far * (1 - their_core)
        there = member_of((y + 2 * half) % 4, (z + dz) % 4, (x + dx) % 4, their_core)
        rows = pl.ds(pl.multiple_of(there * OWN_TOKENS, OWN_TOKENS), OWN_TOKENS)
        pltpu.make_async_copy(hidden_ref.at[rows], hidden.at[place], hidden_sem).start()
        return carry

    lax.fori_loop(0, MEMBERS, load_hidden, 0)

    before, after = slot(0, 0, 3, 0), slot(0, 0, 1, 0)
    for part in parts:
        arrived(before, part)
        send_tokens(tokens.at[before], slot(0, 0, 3, 1), part, other_plane)
        if part % 2 == 0:
            send_tokens(tokens.at[before], slot(0, 0, 2, 0), part, near_plus)
        arrived(after, part)
        send_tokens(tokens.at[after], slot(0, 0, 1, 1), part, other_plane)
        if part % 2 == 1:
            send_tokens(tokens.at[after], slot(0, 0, 2, 0), part, near_minus)
        spread(tokens.at[before], 3, 0, part)
        spread(tokens.at[after], 1, 0, part)
    for part in parts:
        arrived(slot(0, 0, 0, 1), part)
        spread(tokens.at[slot(0, 0, 0, 1)], 0, 1, part)
    place = slot(0, 0, 2, 0)
    for part in parts:
        arrived(place, part)
        send_tokens(tokens.at[place], slot(0, 0, 2, 1), part, other_plane)
        spread(tokens.at[place], 2, 0, part)
    for near in (3, 1, 2):
        place = slot(0, 0, near, 1)
        for part in parts:
            arrived(place, part)
            spread(tokens.at[place], near, 1, part)

    def forward(far):
        depth = 1024
        for part in range(8):
            cols = pl.ds(part * depth, depth)
            rows = tokens[pl.ds(far * 16, 16), :, cols].reshape(256, depth)
            gate_part = jnp.dot(rows, weights[0, cols, :], preferred_element_type=jnp.float32)
            up_part = jnp.dot(rows, weights[1, cols, :], preferred_element_type=jnp.float32)
            if part == 0:
                gate_sum[...] = gate_part
                up_sum[...] = up_part
            else:
                gate_sum[...] += gate_part
                up_sum[...] += up_part
        upstream = hidden[pl.ds(far * 16, 16)].reshape(256, 256).astype(jnp.float32)
        d_gate, d_up = cotangents(gate_sum[...], up_sum[...], upstream)
        cotangent[pl.ds(far * 256, 256), 0:256] = d_gate
        cotangent[pl.ds(far * 256, 256), 256:512] = d_up

    own_tokens.wait()
    loads[0].wait()
    loads[1].wait()
    pltpu.make_async_copy(hidden, hidden, hidden_sem).wait()
    def all_from_other_core(far):
        for near in range(4):
            for half in range(2):
                for part in parts:
                    arrived(slot(far, 1, near, half), part)

    all_from_other_core(0)
    forward(0)
    order = [(0, 0), (0, 1), (1, 0), (3, 0), (1, 1), (3, 1), (2, 0), (2, 1)]
    for near, half in order:
        before, after = slot(3, 0, near, half), slot(1, 0, near, half)
        for part in parts:
            arrived(before, part)
            if half == 0:
                send_tokens(tokens.at[before], slot(2, 0, near, 0), part, far_plus)
            send_tokens(tokens.at[before], slot(3, 1, near, half), part, other_core)
            arrived(after, part)
            if half == 1:
                send_tokens(tokens.at[after], slot(2, 0, near, 1), part, far_minus)
            send_tokens(tokens.at[after], slot(1, 1, near, half), part, other_core)
    for far in (3, 1):
        all_from_other_core(far)
        forward(far)
    for near, half in order:
        place = slot(2, 0, near, half)
        for part in parts:
            arrived(place, part)
            send_tokens(tokens.at[place], slot(2, 1, near, half), part, other_core)
    all_from_other_core(2)
    pl.semaphore_signal(
        ready, inc=1, device_id=(above % 2, member_of(above, z, x, core)), device_id_type=BY_MESH
    )
    forward(2)
    pl.semaphore_wait(ready, 1)

    def send_sums(matrix, step):
        there_island, there = partner(step)
        number = there_island * MEMBERS + there

        @pl.when(number != me)
        def _():
            pltpu.make_async_remote_copy(
                src_ref=outgoing.at[matrix, pl.ds(number * 2, 2)],
                dst_ref=received[matrix].at[pl.ds(me * 2, 2)],
                send_sem=sums_sent,
                recv_sem=sums_got.at[matrix],
                device_id=(there_island, there),
                device_id_type=BY_MESH,
            ).start()

    def backward(matrix):
        def group_of_chips(group, carry):
            steps = [((group * 4 + k) * CHIP_STRIDE) % CHIPS for k in range(4)]
            chips = []
            for step in steps:
                there_island, there = partner(step * 2)
                chips.append(there_island * 32 + there // 2)
            columns = [
                tokens[:, :, pl.ds(pl.multiple_of(chip * BLOCK, BLOCK), BLOCK)].reshape(1024, BLOCK)
                for chip in chips
            ]
            summed = lax.dot_general(
                jnp.concatenate(columns, axis=1),
                cotangent[:, matrix * 256 : (matrix + 1) * 256],
                (((0,), (0,)), ((), ())),
                preferred_element_type=jnp.float32,
            )
            scaled = (inner_rate * summed).astype(jnp.bfloat16)
            for k in range(4):
                for half in range(2):
                    first = k * BLOCK + half * ROWS
                    for block in range(2):
                        outgoing[matrix, (chips[k] * 2 + half) * 2 + block] = scaled[
                            first : first + ROWS, block * BLOCK : (block + 1) * BLOCK
                        ]
            for k in range(4):
                send_sums(matrix, steps[k] * 2 + k % 2)
            return carry

        def other_cores(index, carry):
            send_sums(matrix, ((index * CHIP_STRIDE) % CHIPS) * 2 + (index + 1) % 2)
            return carry

        lax.fori_loop(0, CHIPS // 4, group_of_chips, 0)
        lax.fori_loop(0, CHIPS, other_cores, 0)
        received[matrix][pl.ds(me * 2, 2)] = outgoing[matrix, pl.ds(me * 2, 2)]

    backward(0)
    backward(1)
    loads[2].wait()

    mine = pl.ds(pl.multiple_of(me * ROWS, ROWS), ROWS)
    others = pl.ds(0, (PEERS - 1) * 2)
    all_others = [received[matrix].at[others] for matrix in range(2)]
    outs = (gate_out, up_out)

    def outer_step(matrix):
        def one_block(block, carry):
            first = inverse_ref[0, block]
            second = inverse_ref[1, block]
            cols = pl.ds(pl.multiple_of(block * BLOCK, BLOCK), BLOCK)
            one = received[matrix][first].astype(jnp.float32)
            two = received[matrix][second].astype(jnp.float32)
            average = (one + two) * (1.0 / ISLANDS)
            state = momentum_decay * momentum_out[matrix, :, cols].astype(jnp.float32) + average
            momentum_out[matrix, :, cols] = state.astype(jnp.bfloat16)
            update[matrix, block] = (outer_rate * (average + momentum_decay * state)).astype(
                jnp.bfloat16
            )
            return carry

        lax.fori_loop(0, PEERS, one_block, 0)

    def give_back(matrix):
        def stage(number, there_island, there):
            rows = pl.ds(pl.multiple_of(number * ROWS, ROWS), ROWS)
            for half in range(2):
                block = layout_ref[there_island, there * 2 + half]
                weights[matrix, rows, half * BLOCK : (half + 1) * BLOCK] = update[matrix, block]
            return rows

        def one_device(index, carry):
            there_island, there = partner((index * STRIDE) % PEERS)
            rows = stage(there_island * MEMBERS + there, there_island, there)
            pltpu.make_async_remote_copy(
                src_ref=weights.at[matrix, rows],
                dst_ref=outs[matrix].at[mine],
                send_sem=updates_sent,
                recv_sem=updates_got.at[matrix],
                device_id=(there_island, there),
                device_id_type=BY_MESH,
            ).start()
            return carry

        lax.fori_loop(1, PEERS, one_device, 0)
        stage(me, island, member)
        pltpu.make_async_copy(weights.at[matrix, mine], outs[matrix].at[mine], own_sem.at[matrix]).start()

    for matrix in range(2):
        pltpu.make_async_copy(all_others[matrix], all_others[matrix], sums_got.at[matrix]).wait()
        outer_step(matrix)
        give_back(matrix)

    sent = tokens.at[pl.ds(0, 63)]
    pltpu.make_async_copy(sent, sent, gather_sent).wait()
    for matrix in range(2):
        pltpu.make_async_copy(all_others[matrix], all_others[matrix], sums_sent).wait()
    for matrix in range(2):
        pltpu.make_async_copy(weights.at[matrix, mine], outs[matrix].at[mine], own_sem.at[matrix]).wait()
        part = outs[matrix].at[pl.ds(0, (PEERS - 1) * ROWS)]
        pltpu.make_async_copy(part, part, updates_got.at[matrix]).wait()
        pltpu.make_async_copy(part, part, updates_sent).wait()


def shards(tokens, hidden_grad, gate_weight, up_weight, momentum, layouts):
    blocks = layouts.shape[1]
    places = jnp.arange(blocks, dtype=jnp.int32)
    hit = layouts[:, :, None] == places[None, None, :]
    lies = jnp.arange(ISLANDS * blocks, dtype=jnp.int32).reshape(ISLANDS, blocks)
    inverse = jnp.sum(jnp.where(hit, lies[:, :, None], 0), axis=1, dtype=jnp.int32)
    anywhere = pl.BlockSpec(memory_space=pl.ANY)
    vmem = pl.BlockSpec(memory_space=pltpu.VMEM)
    scalars = pl.BlockSpec(memory_space=pltpu.SMEM)
    bf16 = jnp.bfloat16
    gate, up, state = pl.pallas_call(
        kernel,
        out_shape=(
            pltpu.VMEM((8192, 256), bf16),
            pltpu.VMEM((8192, 256), bf16),
            pltpu.VMEM((2, ROWS, 16384), bf16),
        ),
        in_specs=[anywhere] * 5 + [scalars] * 2,
        out_specs=(vmem, vmem, vmem),
        scratch_shapes=[
            pltpu.VMEM((MEMBERS, OWN_TOKENS, 8192), bf16),
            pltpu.VMEM((2, 8192, 256), bf16),
            pltpu.VMEM((MEMBERS, OWN_TOKENS, 256), bf16),
            pltpu.VMEM((1024, 512), bf16),
            pltpu.VMEM((2, PEERS * 2, ROWS, BLOCK), bf16),
            pltpu.VMEM((PEERS * 2, ROWS, BLOCK), bf16),
            pltpu.VMEM((PEERS * 2, ROWS, BLOCK), bf16),
            pltpu.VMEM((2, PEERS, ROWS, BLOCK), bf16),
            pltpu.VMEM((256, 256), jnp.float32),
            pltpu.VMEM((256, 256), jnp.float32),
            pltpu.SemaphoreType.DMA((3,)),
            pltpu.SemaphoreType.DMA,
            pltpu.SemaphoreType.DMA,
            pltpu.SemaphoreType.DMA,
            pltpu.SemaphoreType.DMA((128,)),
            pltpu.SemaphoreType.DMA,
            pltpu.SemaphoreType.DMA((2,)),
            pltpu.SemaphoreType.DMA((2,)),
            pltpu.SemaphoreType.DMA,
            pltpu.SemaphoreType.DMA((2,)),
            pltpu.SemaphoreType.REGULAR,
        ],
        compiler_params=pltpu.CompilerParams(
            collective_id=0, has_side_effects=True, vmem_limit_bytes=49 * 2**20
        ),
    )(tokens[0], hidden_grad[0], gate_weight[0], up_weight[0], momentum, layouts, inverse)
    return gate[None], up[None], state


def solution(mesh):
    placed = (
        P("island", "fsdp", None),
        P("island", None, "fsdp"),
        P("island", None, "fsdp"),
        P("island", None, "fsdp"),
        P(None, ("island", "fsdp"), None),
        P(),
    )
    return jax.shard_map(
        shards,
        mesh=mesh,
        in_specs=placed,
        out_specs=(
            P("island", None, "fsdp"),
            P("island", None, "fsdp"),
            P(None, ("island", "fsdp"), None),
        ),
        check_vma=False,
    )
```
